256 devices in a mesh: dp: 8 (over z), row: 16 (over y, x), col: 2 (over core).
Axes of the slice: x: 4, y: 4, z: 8, core: 2. Of those that a mesh axis runs over, the one named last changes fastest.
Arguments:
- inputs: bfloat16 [4096, 8192], P('dp', 'row'), may hold values from -6 to 6
- frozen: bfloat16 [8192, 14336], P('row', 'col'), may hold values from -0.0625 to 0.0625
- factor_b: bfloat16 [8192, 64], P('row'), may hold values from -0.0625 to 0.0625
- factor_a: bfloat16 [64, 14336], P(None, 'col'), may hold values from -0.75 to 0.75
- magnitude: float32 [14336], P('col'), may hold values from 0.5 to 2
- cotangent: bfloat16 [4096, 14336], P('dp', 'col'), may hold values from -6 to 6
Outputs:
- mixed: bfloat16 [4096, 14336], P(('dp', 'row'), 'col')
- input_grad: bfloat16 [4096, 8192], P('dp', ('row', 'col'))
- a_grad: float32 [64, 14336], P(None, 'col')
- b_grad: float32 [8192, 64], P('row')
- magnitude_grad: float32 [14336], P('col')
The draws below stay inside these ranges and needn't reach their ends.
All inputs are finite; a program needn't handle non-finite values.
Results may differ from the reference program's by a relative error of at most 0.0055.
Values may be sent and summed in bfloat16 or wider, within the bound.
A program may use at most 128 MiB of HBM per device.

```python
import math
import jax
import jax.numpy as jnp
from jax import lax

D = 8192
FF = 14336
R = 64
TOKENS = 4096
N_COL = 2


def shard_levels(rng, dims, cuts, low, top_value):
    level = 1.0
    for dim, parts in cuts:
        steps = jax.random.uniform(jax.random.fold_in(jax.random.fold_in(rng, 6), dim), (parts,), jnp.float32, low / len(cuts), top_value / len(cuts))
        level = level * jnp.repeat(jnp.exp(steps), dims[dim] // parts).reshape((-1,) + (1,) * (len(dims) - 1 - dim))
    return level


def normal_values(own_key, shape, deviation, most, cuts=(), kind=jnp.bfloat16):
    array = jax.random.normal(own_key, shape, jnp.float32) * deviation
    if len(cuts) > 0:
        array = shard_levels(own_key, shape, cuts, -0.22, 0.18) * array
    return jnp.clip(array, min=-most, max=most).astype(kind)


def setup_inputs(seed: int = 0) -> dict:
    streams_of = jax.random.split(jax.random.key(seed), 7)
    return {
        "inputs": normal_values(streams_of[0], (TOKENS, D), 1.0, 6.0, ((0, 8), (1, 16))),
        "frozen": normal_values(streams_of[1], (D, FF), D ** -0.5, 0.0625, ((0, 16), (1, 2))),
        "factor_b": normal_values(streams_of[2], (D, R), D ** -0.5, 0.0625, ((0, 16),)),
        "factor_a": normal_values(streams_of[3], (R, FF), R ** -0.5, 0.75, ((1, 2),)),
        "magnitude": jnp.clip(jnp.exp(math.log(2.0) - 1.3862944 * jax.random.uniform(streams_of[4], (FF,), jnp.float32) ** shard_levels(streams_of[4], (FF,), ((0, 2),), -0.2, 0.2)), 0.5, 2.0),
        "cotangent": normal_values(streams_of[5], (TOKENS, FF), 1.0, 6.0, ((0, 8), (1, 2))),
    }


def reference(inputs, frozen, factor_b, factor_a, magnitude, cotangent):
    highest = lax.Precision.HIGHEST
    adapted = frozen.astype(jnp.float32) + jnp.dot(factor_b, factor_a, preferred_element_type=jnp.float32)
    column_norm = jnp.sqrt(lax.optimization_barrier(jnp.sum(adapted * adapted, axis=0)) + 1e-06)
    scale = magnitude / column_norm
    factor_wide = factor_a.astype(jnp.float32)
    projected = jnp.dot(inputs, factor_b, preferred_element_type=jnp.float32)
    pre = jnp.dot(inputs, frozen, preferred_element_type=jnp.float32) + jnp.dot(projected, factor_wide, precision=highest)
    mixed = (pre * scale).astype(jnp.bfloat16)
    grad_pre = cotangent.astype(jnp.float32) * scale
    grad_low = grad_pre.astype(jnp.bfloat16)
    block_width = FF // N_COL
    grad_blocks = grad_pre.reshape(grad_pre.shape[0], N_COL, block_width)
    factor_blocks = factor_wide.reshape(factor_wide.shape[0], N_COL, block_width)
    up_blocks = jnp.einsum('tcf,rcf->ctr', grad_blocks, factor_blocks, precision=highest)
    up_rounded = lax.optimization_barrier(up_blocks.astype(jnp.bfloat16))
    upstream = lax.optimization_barrier(jnp.sum(up_rounded.astype(jnp.float32), axis=0)).astype(jnp.bfloat16)
    input_grad = (jnp.dot(grad_low, frozen.T, preferred_element_type=jnp.float32) + jnp.dot(upstream, factor_b.T, preferred_element_type=jnp.float32)).astype(jnp.bfloat16)
    a_grad = jnp.dot(projected.T, grad_pre, precision=highest)
    b_grad = jnp.dot(inputs.T, upstream, preferred_element_type=jnp.float32)
    magnitude_grad = lax.optimization_barrier(jnp.sum(cotangent.astype(jnp.float32) * pre, axis=0)) / column_norm
    return (mixed, input_grad, a_grad, b_grad, magnitude_grad)
```

```python
import functools

import jax
import jax.numpy as jnp
from jax import lax
from jax.experimental import pallas as pl
from jax.experimental.pallas import tpu as pltpu
from jax.sharding import PartitionSpec as P

MESH = pl.DeviceIdType.MESH
F32 = jnp.float32
BF16 = jnp.bfloat16
CHUNKS = 8
SIDE = 4
DEPTH = 8


def wrap(value, size):
    return lax.rem(value, size)


def kernel(
    x_ref, f_hbm, b_ref, a_ref, g_ref, c_hbm,
    mixed_ref, ig_ref, ag_ref, bg_ref, mg_ref, sc_ref,
    fro, cot, part, s1r, s2r, sums, s3r, s4r,
    nx, ny, mx, my, mz, norm,
    prs, prx, pry, prg, pbf,
    asend, arecv, agf,
    iga, igr, upacc, ups, upr, bs, br, bg,
    fsem, csem,
    s1s, s1q, s2s, s2q, s3s, s3q, s4s, s4q,
    nxs, nxq, nys, nyq, mxs, mxq, mys, myq, mzs, mzq,
    p1s, p1q, p2s, p2q, p3s, p3q,
    ars, arq, azs, azq, axs, axq, ays, ayq,
    sib_s, sib_q, brs, brq, bgs, bgq,
):
    W = fro.shape[2]
    r = lax.axis_index("row")
    z = lax.axis_index("dp")
    k = lax.axis_index("col")
    x = lax.rem(r, SIDE)
    y = lax.div(r, SIDE)

    def at_x(p):
        return {"row": y * SIDE + p}

    def at_y(p):
        return {"row": p * SIDE + x}

    def at_z(p):
        return {"dp": p}

    sibling = {"col": 1 - k}
    first = ((x, at_x), (y, at_y))
    second = ((y, at_y), (x, at_x))

    def cols(c):
        return pl.ds(pl.multiple_of(c * W, 128), W)

    def rcopy(src, dst, ss, rs, dev):
        return pltpu.make_async_remote_copy(
            src_ref=src, dst_ref=dst, send_sem=ss, recv_sem=rs,
            device_id=dev, device_id_type=MESH,
        )

    def f_copy(c):
        return pltpu.make_async_copy(f_hbm.at[:, cols(c)], fro.at[c], fsem.at[c])

    def c_copy(c):
        return pltpu.make_async_copy(c_hbm.at[:, cols(c)], cot.at[c], csem.at[c])

    def near(pos, d):
        return wrap(pos + (1 if d == 0 else SIDE - 1), SIDE)

    def s1(kind, c, d):
        pos, dev = first[kind]
        return rcopy(
            part.at[c, wrap(pos + 2, SIDE), pl.ds(2 * d, 2)], s1r.at[c, d],
            s1s.at[c, d], s1q.at[c, d], dev(near(pos, d)),
        )

    def s2(kind, c, d):
        pos, dev = first[kind]
        return rcopy(
            part.at[c, near(pos, d)], s2r.at[c, d],
            s2s.at[c, d], s2q.at[c, d], dev(near(pos, d)),
        )

    def s3(kind, c, d):
        pos, dev = second[kind]
        return rcopy(
            sums.at[c, wrap(pos + 2, SIDE), pl.ds(16 * d, 16)], s3r.at[c, d],
            s3s.at[c, d], s3q.at[c, d], dev(near(pos, d)),
        )

    def s4(kind, c, d):
        pos, dev = second[kind]
        return rcopy(
            sums.at[c, near(pos, d)], s4r.at[c, d],
            s4s.at[c, d], s4q.at[c, d], dev(near(pos, d)),
        )

    def t1(i):
        for kind in (0, 1):
            for d in (0, 1):
                s1(kind, 2 * i + kind, d).start()

    def t2(i):
        for kind in (0, 1):
            c = 2 * i + kind
            pos, _ = first[kind]
            for d in (0, 1):
                s1(kind, c, d).wait_recv()
                nb = near(pos, d)
                rows = pl.ds(2 * d, 2)
                part[c, nb, rows] = (
                    part[c, nb, rows].astype(F32) + s1r[c, d].astype(F32)
                ).astype(BF16)
                s2(kind, c, d).start()

    def t3(i):
        for kind in (0, 1):
            c = 2 * i + kind
            pos, _ = first[kind]
            for d in (0, 1):
                s2(kind, c, d).wait_recv()
            for j in range(SIDE):
                sums[c, j] = (
                    part[c, pos, j].astype(F32) + s2r[c, 0, j].astype(F32)
                    + s2r[c, 1, j].astype(F32)
                ).astype(BF16)
            for d in (0, 1):
                s3(kind, c, d).start()

    def t4(i):
        for kind in (0, 1):
            c = 2 * i + kind
            pos, _ = second[kind]
            for d in (0, 1):
                s3(kind, c, d).wait_recv()
                nb = near(pos, d)
                rows = pl.ds(16 * d, 16)
                sums[c, nb, rows] = (
                    sums[c, nb, rows].astype(F32) + s3r[c, d].astype(F32)
                ).astype(BF16)
                s4(kind, c, d).start()

    def t5(i):
        for kind in (0, 1):
            c = 2 * i + kind
            pos, _ = first[kind]
            own, _ = second[kind]
            for d in (0, 1):
                s4(kind, c, d).wait_recv()
            pre = (
                part[c, pos, own].astype(F32) + s2r[c, 0, own].astype(F32)
                + s2r[c, 1, own].astype(F32)
                + s4r[c, 0].astype(F32) + s4r[c, 1].astype(F32)
            )
            mixed_ref[:, cols(c)] = (pre * sc_ref[pl.ds(c, 1), :]).astype(BF16)

    def gather(buf, pos, size, dev, ss, rs):
        return [
            rcopy(buf.at[pos], buf.at[pos], ss.at[d], rs.at[d], dev(wrap(pos + d, size)))
            for d in range(1, size)
        ]

    norm_x = gather(nx, x, SIDE, at_x, nxs, nxq)
    norm_y = gather(ny, y, SIDE, at_y, nys, nyq)
    mag_x = gather(mx, x, SIDE, at_x, mxs, mxq)
    mag_y = gather(my, y, SIDE, at_y, mys, myq)
    mag_z = gather(mz, z, DEPTH, at_z, mzs, mzq)
    proj_x = [
        rcopy(prs.at[wrap(x + d, SIDE)], prx.at[x], p1s.at[d], p1q.at[d], at_x(wrap(x + d, SIDE)))
        for d in range(1, SIDE)
    ]
    proj_y = gather(pry, y, SIDE, at_y, p2s, p2q)
    proj_g = gather(prg, x, SIDE, at_x, p3s, p3q)
    a_part = [
        rcopy(asend.at[wrap(z + d, DEPTH)], arecv.at[z], ars.at[d], arq.at[d], at_z(wrap(z + d, DEPTH)))
        for d in range(1, DEPTH)
    ]
    kz = lax.rem(z, 2)
    iz = lax.div(z, 2)
    pz = x + kz * (y - x)
    a_z = [
        rcopy(agf.at[kz, pz, iz], agf.at[kz, pz, iz], azs.at[d], azq.at[d], at_z(wrap(z + d, DEPTH)))
        for d in range(1, DEPTH)
    ]
    a_x = gather(agf.at[0], x, SIDE, at_x, axs, axq)
    a_y = gather(agf.at[1], y, SIDE, at_y, ays, ayq)
    b_part = [
        rcopy(bs.at[wrap(z + d, DEPTH)], br.at[z], brs.at[d], brq.at[d], at_z(wrap(z + d, DEPTH)))
        for d in range(1, DEPTH)
    ]
    b_z = gather(bg, z, DEPTH, at_z, bgs, bgq)
    up_x = rcopy(ups, upr, sib_s.at[0], sib_q.at[0], sibling)
    ig_x = rcopy(iga.at[1 - k], igr, sib_s.at[1], sib_q.at[1], sibling)

    def start(copies):
        for copy in copies:
            copy.start()

    def wait(copies):
        for copy in copies:
            copy.wait_recv()

    def total(buf, count):
        value = buf[0].astype(F32)
        for j in range(1, count):
            value = value + buf[j].astype(F32)
        return value

    for c in (0, 1):
        f_copy(c).start()
    for c in (0, 1):
        c_copy(c).start()

    @pl.loop(2, CHUNKS)
    def _(c):
        f_copy(c).start()

    @pl.loop(2, CHUNKS)
    def _(c):
        c_copy(c).start()

    barrier = pltpu.get_barrier_semaphore()
    for d in range(1, SIDE):
        for dev in (at_x(wrap(x + d, SIDE)), at_y(wrap(y + d, SIDE))):
            pl.semaphore_signal(barrier, inc=1, device_id=dev, device_id_type=MESH)
    for d in range(1, DEPTH):
        pl.semaphore_signal(barrier, inc=1, device_id=at_z(wrap(z + d, DEPTH)), device_id_type=MESH)
    pl.semaphore_signal(barrier, inc=1, device_id=sibling, device_id_type=MESH)

    low = jnp.dot(x_ref[...], b_ref[...], preferred_element_type=F32).T
    for q in range(SIDE):
        prs[q] = low[:, 128 * q:128 * (q + 1)]
    prx[x] = prs[x]

    def adapt(c):
        f_copy(c).wait()
        square = jnp.zeros((1, W), F32)
        for kb in range(4):
            rows = pl.ds(128 * kb, 128)
            value = fro[c, rows, :].astype(F32) + jnp.dot(
                b_ref[rows, :], a_ref[:, cols(c)], preferred_element_type=F32
            )
            square = square + jnp.sum(value * value, axis=0, keepdims=True)
            fro[c, rows, :] = value.astype(BF16)
        nx[x, pl.ds(c, 1), :] = square

    def products(i):
        for kind in (0, 1):
            c = 2 * i + kind
            c_copy(c).wait()
            value = jnp.dot(x_ref[...], fro[c], preferred_element_type=F32)
            mx[x, pl.ds(c, 1), :] = jnp.sum(
                value * cot[c].astype(F32), axis=0, keepdims=True
            )
            low = value.astype(BF16)
            for yy in range(SIDE):
                for xx in range(SIDE):
                    t = 32 * (SIDE * yy + xx)
                    where = (c, xx, yy) if kind == 0 else (c, yy, xx)
                    part[where] = low[t:t + 32]

    adapt(0)
    adapt(1)
    products(0)
    pl.semaphore_wait(barrier, 2 * (SIDE - 1) + DEPTH)
    start(proj_x)
    t1(0)

    @pl.loop(2, CHUNKS)
    def _(c):
        adapt(c)

    start(norm_x)

    @pl.loop(1, 4)
    def _(i):
        products(i)
        t1(i)

        @pl.when(i == 1)
        def _():
            wait(proj_x)
            pry[y] = total(prx, SIDE)
            start(proj_y)
            wait(norm_x)
            ny[y] = total(nx, SIDE)
            start(norm_y)

        @pl.when(i == 2)
        def _():
            wait(proj_y)
            prg[x] = total(pry, SIDE).astype(BF16)
            start(proj_g)
            wait(norm_y)
            size = jnp.sqrt(total(ny, SIDE) + 1e-06)
            norm[...] = size
            sc_ref[...] = g_ref[...] / size

        t2(i - 1)

    start(mag_x)
    wait(proj_g)
    for q in range(SIDE):
        for j in range(SIDE):
            pbf[j, :, 128 * q:128 * (q + 1)] = prg[q, 16 * j:16 * (j + 1), :]

    @pl.loop(0, 4)
    def _(i):
        for kind in (0, 1):
            c = 2 * i + kind
            pos, _ = first[kind]
            asend[c] = jnp.dot(pbf[pos], cot[c], preferred_element_type=F32).astype(BF16)

    start(a_part)
    arecv[z] = asend[z]
    t2(3)
    wait(mag_x)
    my[y] = total(mx, SIDE)
    start(mag_y)
    t3(0)

    iga[...] = jnp.zeros_like(iga)
    upacc[...] = jnp.zeros_like(upacc)

    contract = (((1,), (1,)), ((), ()))

    def grads(c):
        grad = (cot[c].astype(F32) * sc_ref[pl.ds(c, 1), :]).astype(BF16)
        for h in (0, 1):
            iga[h] += lax.dot_general(
                grad, fro[c, pl.ds(256 * h, 256), :], contract, preferred_element_type=F32
            )
        upacc[...] += lax.dot_general(
            grad, a_ref[:, cols(c)], contract, preferred_element_type=F32
        )

    @pl.loop(0, 4)
    def _(i):
        @pl.loop(0, 2)
        def _(kind):
            grads(2 * i + kind)

        @pl.when(i == 0)
        def _():
            wait(a_part)
            agf[kz, pz, iz] = total(arecv, DEPTH).astype(BF16)
            start(a_z)
            wait(mag_y)
            mz[z] = total(my, SIDE)
            start(mag_z)

        @pl.when(i == 2)
        def _():
            wait(a_z)
            start(a_x)
            start(a_y)

        @pl.when(i < 3)
        def _():
            t3(i + 1)

        @pl.when(i == 3)
        def _():
            ups[...] = upacc[...].astype(BF16)
            up_x.start()
            ig_x.start()

        t4(i)

    up_x.wait_recv()
    up = (ups[...].astype(F32) + upr[...].astype(F32)).astype(BF16)
    bt = lax.dot_general(up, x_ref[...], (((0,), (0,)), ((), ())), preferred_element_type=F32)
    for j in range(DEPTH):
        bs[j] = bt[8 * j:8 * (j + 1), :]
    br[z] = bs[z]
    start(b_part)

    @pl.loop(0, 2)
    def _(i):
        t5(i)

    ig_x.wait_recv()
    ig_ref[...] = (iga[k] + igr[...]).astype(BF16)
    wait(b_part)
    bg[z] = total(br, DEPTH)
    start(b_z)

    @pl.loop(2, 4)
    def _(i):
        t5(i)

    wait(a_x)
    wait(a_y)
    for kind in (0, 1):
        for j in range(SIDE):
            for i in range(4):
                ag_ref[16 * j:16 * (j + 1), W * (2 * i + kind):W * (2 * i + kind + 1)] = agf[kind, j, i]
    wait(mag_z)
    mg_ref[...] = total(mz, DEPTH) / norm[...]
    wait(b_z)
    for j in range(DEPTH):
        bg_ref[8 * j:8 * (j + 1), :] = bg[j]

    @pl.loop(0, 4)
    def _(i):
        for kind in (0, 1):
            for d in (0, 1):
                for send in (s1, s2, s3, s4):
                    send(kind, 2 * i + kind, d).wait_send()

    for copies in (
        norm_x, norm_y, mag_x, mag_y, mag_z, proj_x, proj_y, proj_g,
        a_part, a_z, a_x, a_y, b_part, b_z, [up_x, ig_x],
    ):
        for copy in copies:
            copy.wait_send()


def body(inputs, frozen, factor_b, factor_a, magnitude, cotangent):
    tokens, depth = inputs.shape
    width = frozen.shape[1]
    rank = factor_a.shape[0]
    W = width // CHUNKS
    share = tokens // (SIDE * SIDE)
    quarter = tokens // SIDE
    dma = pltpu.SemaphoreType.DMA
    scratch = [
        pltpu.VMEM((CHUNKS, depth, W), BF16),
        pltpu.VMEM((CHUNKS, tokens, W), BF16),
        pltpu.VMEM((CHUNKS, SIDE, SIDE, share, W), BF16),
        pltpu.VMEM((CHUNKS, 2, 2, share, W), BF16),
        pltpu.VMEM((CHUNKS, 2, SIDE, share, W), BF16),
        pltpu.VMEM((CHUNKS, SIDE, share, W), BF16),
        pltpu.VMEM((CHUNKS, 2, share // 2, W), BF16),
        pltpu.VMEM((CHUNKS, 2, share, W), BF16),
        pltpu.VMEM((SIDE, CHUNKS, W), F32),
        pltpu.VMEM((SIDE, CHUNKS, W), F32),
        pltpu.VMEM((SIDE, CHUNKS, W), F32),
        pltpu.VMEM((SIDE, CHUNKS, W), F32),
        pltpu.VMEM((DEPTH, CHUNKS, W), F32),
        pltpu.VMEM((CHUNKS, W), F32),
        pltpu.VMEM((SIDE, rank, quarter), F32),
        pltpu.VMEM((SIDE, rank, quarter), F32),
        pltpu.VMEM((SIDE, rank, quarter), F32),
        pltpu.VMEM((SIDE, rank, quarter), BF16),
        pltpu.VMEM((SIDE, rank // SIDE, tokens), BF16),
        pltpu.VMEM((CHUNKS, rank // SIDE, W), BF16),
        pltpu.VMEM((DEPTH, rank // SIDE, W), BF16),
        pltpu.VMEM((2, SIDE, CHUNKS // 2, rank // SIDE, W), BF16),
        pltpu.VMEM((2, tokens, depth // 2), F32),
        pltpu.VMEM((tokens, depth // 2), F32),
        pltpu.VMEM((tokens, rank), F32),
        pltpu.VMEM((tokens, rank), BF16),
        pltpu.VMEM((tokens, rank), BF16),
        pltpu.VMEM((DEPTH, rank // DEPTH, depth), F32),
        pltpu.VMEM((DEPTH, rank // DEPTH, depth), F32),
        pltpu.VMEM((DEPTH, rank // DEPTH, depth), F32),
        dma((CHUNKS,)), dma((CHUNKS,)),
    ]
    scratch += [dma((CHUNKS, 2))] * 8
    scratch += [dma((SIDE,))] * 8 + [dma((DEPTH,))] * 2
    scratch += [dma((SIDE,))] * 6
    scratch += [dma((DEPTH,))] * 4 + [dma((SIDE,))] * 4
    scratch += [dma((2,))] * 2 + [dma((DEPTH,))] * 4
    vmem = pl.BlockSpec(memory_space=pltpu.VMEM)
    hbm = pl.BlockSpec(memory_space=pl.ANY)
    mixed, ig, ag, bt, mg, scale = pl.pallas_call(
        kernel,
        out_shape=(
            jax.ShapeDtypeStruct((share, width), BF16),
            jax.ShapeDtypeStruct((tokens, depth // 2), BF16),
            jax.ShapeDtypeStruct((rank, width), BF16),
            jax.ShapeDtypeStruct((rank, depth), F32),
            jax.ShapeDtypeStruct((CHUNKS, W), F32),
            jax.ShapeDtypeStruct((CHUNKS, W), F32),
        ),
        in_specs=[vmem, hbm, vmem, vmem, vmem, hbm],
        out_specs=(vmem,) * 6,
        scratch_shapes=scratch,
        compiler_params=pltpu.CompilerParams(
            collective_id=0, has_side_effects=True, vmem_limit_bytes=60 * 1024 * 1024
        ),
    )(inputs, frozen, factor_b, factor_a, magnitude.reshape(CHUNKS, W), cotangent)
    a_grad = ag.astype(F32) * scale.reshape(1, width)
    return (mixed, ig, a_grad, bt.T, mg.reshape(width))


def solution(mesh):
    return jax.shard_map(
        body,
        mesh=mesh,
        in_specs=(
            P("dp", "row"),
            P("row", "col"),
            P("row", None),
            P(None, "col"),
            P("col"),
            P("dp", "col"),
        ),
        out_specs=(
            P(("dp", "row"), "col"),
            P("dp", ("row", "col")),
            P(None, "col"),
            P("row", None),
            P("col"),
        ),
        check_vma=False,
    )
```
